512 devices in a mesh: seq: 8 (over y, core), mp: 64 (over z, x).
Axes of the slice: x: 4, y: 4, z: 16, core: 2. Of those that a mesh axis runs over, the one named last changes fastest.
Arguments:
- residual_in: bfloat16 [1024, 8192], P('seq', 'mp'), may hold values from -6 to 6
- ssm_input: bfloat16 [1024, 16384], P('seq', 'mp'), may hold values from -6 to 6
- gate_input: bfloat16 [1024, 16384], P('seq', 'mp'), may hold values from -6 to 6
- b_proj: bfloat16 [1024, 8, 256], P('seq'), may hold values from -6 to 6
- c_proj: bfloat16 [1024, 8, 256], P('seq'), may hold values from -6 to 6
- step_raw: float32 [1024, 256], P('seq', 'mp'), may hold values from -4.2 to 3.5
- decay_log: float32 [256], P('mp'), may hold values from -4.61 to 1.26
- skip_gain: float32 [256], P('mp'), may hold values from 0.5 to 2
- mixer_gain: float32 [16384], replicated, may hold values from 0.1 to 1.9
- out_weight: bfloat16 [16384, 8192], P('seq', 'mp'), may hold values from -0.046875 to 0.046875
- final_gain: float32 [8192], replicated, may hold values from 0.1 to 1.9
- head_weight: bfloat16 [8192, 65536], P('seq', 'mp'), may hold values from -24 to 24
- targets: int32 [1024], replicated, may hold values from 0 to 65535
- segment_ids: int32 [1024], replicated, may hold values from 0 to 1, as said below
- loss_mask: int32 [1024], replicated, may hold values from 0 to 1, as said below
Outputs:
- mixer_out: bfloat16 [1024, 8192], P('seq', 'mp')
- token_logp: float32 [1024], P('seq')
- response_logp: float32 [3], replicated
The draws below stay inside these ranges and needn't reach their ends.
Inputs may be any that keep to these rules, and one draw needn't show every extreme that they name: `segment_ids`: 0 on the positions of the chosen response, then 1 on those of the rejected one; each response holds at least 256 positions. `loss_mask`: 1 at the first position of each response.
All inputs are finite; a program needn't handle non-finite values.
Results may differ from the reference program's by a relative error of at most 0.008.
Values may be sent and summed in bfloat16 or wider, within the bound.
No kernel may reach another device: no remote copies, remote signals or barrier semaphores. Data moves between devices by JAX's collectives and lax.ppermute only.
A program may use at most 64 MiB of HBM per device.

```python
import math
import jax
import jax.numpy as jnp
import numpy as np
from jax import lax

D = 8192
SCAN_HEADS = 256
HEAD_DIM = 64
STATE = 256
GROUPS = 8
VOCAB = 65536
BLOCK = 64
WINDOW_TOKENS = 1024
INNER = 16384


def boundary_of(key):
    return jax.random.randint(key, (), WINDOW_TOKENS // 4, 3 * WINDOW_TOKENS // 4 + 1)


def draw_segment_ids(key, part):
    start_place = boundary_of(key)
    return (jnp.arange(WINDOW_TOKENS) >= start_place).astype(jnp.int32)


def draw_loss_mask(key, part):
    start_place = boundary_of(key)
    key = jax.random.fold_in(key, 12)
    coins = jax.random.randint(key, (WINDOW_TOKENS,), 0, 4)
    places = jnp.arange(WINDOW_TOKENS)
    forced = (places == 0) | (places == start_place)
    return jnp.where(forced | (coins > 0), 1, 0).astype(jnp.int32)


def draw_step_raw(key, part):
    key = jax.random.fold_in(key, 13)
    random_keys = jax.random.split(key, 3)
    base_offset = jax.random.uniform(random_keys[0], (WINDOW_TOKENS, SCAN_HEADS), jnp.float32, -4.0, -3.0)
    group_rows = jax.random.randint(random_keys[1], (WINDOW_TOKENS, 1), 0, 256) == 0
    group_length = jax.random.uniform(random_keys[2], (WINDOW_TOKENS, SCAN_HEADS), jnp.float32, 2.0, 3.5)
    return jnp.where(group_rows, group_length, base_offset)


def draw_decay_log(key, part):
    key = jax.random.fold_in(key, 14)
    random_keys = jax.random.split(key, 3)
    slow_share = 0.5
    slow_heads = jax.random.uniform(random_keys[0], (SCAN_HEADS,), jnp.float32) < slow_share
    slow_rate = jax.random.uniform(random_keys[1], (SCAN_HEADS,), jnp.float32, math.log(0.01), math.log(0.03))
    fast_rate = jax.random.uniform(random_keys[2], (SCAN_HEADS,), jnp.float32, math.log(2.2), math.log(3.5))
    return jnp.where(slow_heads, slow_rate, fast_rate)


def draw_head_weight(key, part):
    key = jax.random.fold_in(key, 15)
    random_keys = jax.random.split(key, 2)
    column_scale = jnp.exp(jax.random.uniform(random_keys[0], (1, VOCAB), jnp.float32, 0.0, math.log(10.0)))
    base_offset = jax.random.normal(random_keys[1], (D, VOCAB), jnp.float32)
    weight = base_offset * column_scale / math.sqrt(D)
    return weight.astype(jnp.bfloat16)


def plant(drawn, key, smallest, high):
    shape = drawn.shape
    spot = [jax.random.randint(jax.random.fold_in(key, axis), (), 0, shape[axis]) for axis in range(len(shape))]
    drawn = drawn.at[tuple(spot)].set(smallest)
    longest = shape.index(max(shape))
    spot[longest] = (spot[longest] + 1) % shape[longest]
    return drawn.at[tuple(spot)].set(high)


def level_of(rng, dims, cuts, least, largest):
    level = 1.0
    for position, parts in cuts:
        steps = jax.random.uniform(jax.random.fold_in(jax.random.fold_in(rng, 6), position), (parts,), jnp.float32, least / len(cuts), largest / len(cuts))
        level = level * jnp.repeat(jnp.exp(steps), dims[position] // parts).reshape((-1,) + (1,) * (len(dims) - 1 - position))
    return level


def rank_bounds(amount, skew):
    loads = [(1 << 20) // math.isqrt(rank ** skew) + 1 for rank in range(1, amount + 1)]
    scale = 1 + sum(loads) // (1 << 30)
    return np.cumsum(np.array([max(1, weight // scale) for weight in loads]))


def ranked(stream_key, extent, amount, skew):
    listing = rank_bounds(amount, skew)
    pick = jax.random.randint(jax.random.fold_in(stream_key, 1), extent, 0, int(listing[amount - 1]))
    rank = jnp.searchsorted(jnp.asarray(listing, jnp.int32), pick, side="right")
    return jax.random.permutation(jax.random.fold_in(stream_key, 2), amount)[rank].astype(jnp.int32)


def centred(own_key, shape, deviation, limit, cuts=(), dtype=jnp.bfloat16):
    values = jax.random.normal(own_key, shape, jnp.float32) * deviation
    if len(cuts) > 0:
        values = level_of(own_key, shape, cuts, -0.22, 0.18) * values
    return jnp.clip(values, min=-limit, max=limit).astype(dtype)


def setup_inputs(seed: int = 0) -> dict:
    key_of = jax.random.split(jax.random.key(seed), 16)
    residual_in = centred(key_of[0], (WINDOW_TOKENS, D), 1.0, 6.0, ((0, 8), (1, 64)))
    ssm_input = centred(key_of[1], (WINDOW_TOKENS, INNER), 1.0, 6.0, ((0, 8), (1, 64)))
    gate_input = centred(key_of[2], (WINDOW_TOKENS, INNER), 1.0, 6.0, ((0, 8), (1, 64)))
    b_proj = centred(key_of[3], (WINDOW_TOKENS, GROUPS, STATE), 1.0, 6.0, ((0, 8),))
    c_proj = centred(key_of[4], (WINDOW_TOKENS, GROUPS, STATE), 1.0, 6.0, ((0, 8),))
    step_raw = draw_step_raw(jax.random.fold_in(key_of[15], 71), 0)
    decay_log = draw_decay_log(jax.random.fold_in(key_of[15], 71), 0)
    skip_gain = jnp.clip(0.5 + 1.5 * jax.random.uniform(key_of[7], (SCAN_HEADS,), jnp.float32) ** level_of(key_of[7], (SCAN_HEADS,), ((0, 64),), -0.2, 0.2), 0.5, 2.0)
    mixer_gain = jnp.clip(1.0 + 0.18 * jax.random.normal(key_of[8], (INNER,), jnp.float32), 0.1, 1.9)
    out_weight = centred(key_of[9], (INNER, D), INNER ** -0.5, 0.046875, ((0, 8), (1, 64)))
    final_gain = jnp.clip(1.0 + 0.18 * jax.random.normal(key_of[10], (D,), jnp.float32), 0.1, 1.9)
    head_weight = draw_head_weight(jax.random.fold_in(key_of[15], 71), 0)
    targets = plant(ranked(key_of[12], (WINDOW_TOKENS,), VOCAB, 2), jax.random.fold_in(key_of[12], 3), 0, VOCAB - 1).astype(jnp.int32)
    segment_ids = draw_segment_ids(jax.random.fold_in(key_of[15], 71), 0)
    loss_mask = draw_loss_mask(jax.random.fold_in(key_of[15], 71), 0)
    return dict(residual_in=residual_in, ssm_input=ssm_input, gate_input=gate_input, b_proj=b_proj, c_proj=c_proj, step_raw=step_raw, decay_log=decay_log, skip_gain=skip_gain, mixer_gain=mixer_gain, out_weight=out_weight, final_gain=final_gain, head_weight=head_weight, targets=targets, segment_ids=segment_ids, loss_mask=loss_mask)


EPS = 1e-05
HIGH = lax.Precision.HIGHEST

def reference(residual_in, ssm_input, gate_input, b_proj, c_proj, step_raw, decay_log, skip_gain, mixer_gain, out_weight, final_gain, head_weight, targets, segment_ids, loss_mask):
    group_lookup = (jnp.arange(SCAN_HEADS) // (SCAN_HEADS // GROUPS)).astype(jnp.int32)
    inputs = ssm_input.astype(jnp.float32).reshape(WINDOW_TOKENS, SCAN_HEADS, HEAD_DIM)
    b_heads = jnp.take(b_proj.astype(jnp.float32), group_lookup, axis=1)
    c_heads = jnp.take(c_proj.astype(jnp.float32), group_lookup, axis=1)
    step_size = jax.nn.softplus(step_raw)
    log_decay = -jnp.exp(decay_log)[None, :] * step_size
    block_count = WINDOW_TOKENS // BLOCK

    def by_block(array):
        return array.reshape((block_count, BLOCK) + array.shape[1:])
    before_place = jnp.maximum(jnp.arange(block_count) * BLOCK - 1, 0).astype(jnp.int32)
    seg_before = segment_ids[before_place]
    places = jnp.arange(BLOCK)

    def block_step(state, pieces):
        x_block, dt_block, ld_block, b_block, c_block, seg_block, seg_prev = pieces
        cumulative = jnp.cumsum(ld_block, axis=0)
        causal = (places[:, None] >= places[None, :]) & (seg_block[:, None] == seg_block[None, :])
        causal_heads = causal[:, :, None]
        gap_log = cumulative[:, None, :] - cumulative[None, :, :]
        weights = jnp.where(causal_heads, jnp.exp(jnp.where(causal_heads, gap_log, 0.0)), 0.0)
        scores = jnp.einsum('thn,shn->tsh', c_block, b_block, precision=HIGH)
        scaled = dt_block[:, :, None] * x_block
        inner_out = jnp.einsum('tsh,shp->thp', scores * weights, scaled, precision=HIGH)
        carry_in = jnp.where((seg_block == seg_prev)[:, None], jnp.exp(cumulative), 0.0)
        outer_out = carry_in[:, :, None] * jnp.einsum('thn,hpn->thp', c_block, state, precision=HIGH)
        to_end = jnp.where((seg_block == seg_block[-1])[:, None], jnp.exp(cumulative[-1][None, :] - cumulative), 0.0)
        added_state = jnp.einsum('sh,shp,shn->hpn', to_end, scaled, b_block, precision=HIGH)
        carry_keep = jnp.where(seg_block[-1] == seg_prev, jnp.exp(cumulative[-1]), 0.0)
        new_state = carry_keep[:, None, None] * state + added_state
        return (new_state, inner_out + outer_out)
    start_state = jnp.zeros((SCAN_HEADS, HEAD_DIM, STATE), jnp.float32)
    pieces = (by_block(inputs), by_block(step_size), by_block(log_decay), by_block(b_heads), by_block(c_heads), by_block(segment_ids), seg_before)
    final_state, block_result = lax.scan(block_step, start_state, pieces)
    ssd = block_result.reshape(WINDOW_TOKENS, SCAN_HEADS, HEAD_DIM) + skip_gain[None, :, None] * inputs
    gated = (ssd.reshape(WINDOW_TOKENS, INNER) * jax.nn.silu(gate_input.astype(jnp.float32))).astype(jnp.bfloat16)
    grouped = gated.astype(jnp.float32).reshape(WINDOW_TOKENS, GROUPS, INNER // GROUPS)
    group_scale = lax.rsqrt(lax.optimization_barrier(jnp.mean(grouped * grouped, axis=2)) + EPS)
    mixer_normed = ((grouped * group_scale[:, :, None]).reshape(WINDOW_TOKENS, INNER) * mixer_gain).astype(jnp.bfloat16)
    mixer_out = jnp.dot(mixer_normed, out_weight, preferred_element_type=jnp.float32).astype(jnp.bfloat16)
    residual_sum = (residual_in.astype(jnp.float32) + mixer_out.astype(jnp.float32)).astype(jnp.bfloat16)
    residual_float = residual_sum.astype(jnp.float32)
    row_scale = lax.rsqrt(lax.optimization_barrier(jnp.mean(residual_float * residual_float, axis=1)) + EPS)
    head_input = (residual_float * row_scale[:, None] * final_gain).astype(jnp.bfloat16)

    def block_logp(pieces_in):
        rows, wanted = pieces_in
        logits = jnp.dot(rows, head_weight, preferred_element_type=jnp.float32)
        top_value = lax.optimization_barrier(jnp.max(logits, axis=1))
        exp_mass = lax.optimization_barrier(jnp.sum(jnp.exp(logits - top_value[:, None]), axis=1))
        picked = jnp.take_along_axis(logits, wanted[:, None], axis=1)[:, 0]
        return picked - (top_value + jnp.log(exp_mass))
    token_logp = lax.map(block_logp, (head_input.reshape(block_count, BLOCK, D), targets.reshape(block_count, BLOCK))).reshape(WINDOW_TOKENS)
    counted = loss_mask == 1
    means = []
    for which in range(2):
        selected = counted & (segment_ids == which)
        total_logp = jnp.sum(jnp.where(selected, token_logp, 0.0))
        count_rows = jnp.sum(selected.astype(jnp.float32))
        means.append(total_logp / count_rows)
    response_logp = jnp.stack([means[0], means[1], means[0] - means[1]])
    return (mixer_out, token_logp, response_logp)
```

```python
import jax
import jax.numpy as jnp
from jax import lax
from jax.experimental import pallas as pl
from jax.experimental.pallas import tpu as pltpu
from jax.sharding import Mesh, PartitionSpec as P

EPS = 1e-05
HIGH = lax.Precision.HIGHEST
F32 = jnp.float32
BF16 = jnp.bfloat16

NY, NC, NG, NL, NX = (4, 2, 8, 2, 4)
NZ = NG * NL
AXES = ("y", "core", "zg", "zl", "x")
SEQ = ("y", "core")
MP = ("zg", "zl", "x")
ROWS = 128
HEADS = 4
WIDTH = 64
CHANNELS = HEADS * WIDTH
STATE = 256
GROUPS = 8
MSG = STATE + 16


def dot(a, b, precision=None):
    return jnp.dot(a, b, preferred_element_type=F32, precision=precision)


def vmem():
    return pl.BlockSpec(memory_space=pltpu.VMEM)


def smem():
    return pl.BlockSpec(memory_space=pltpu.SMEM)


def call(body, out_shape, specs):
    many = isinstance(out_shape, (tuple, list))
    return pl.pallas_call(
        body,
        out_shape=out_shape,
        in_specs=specs,
        out_specs=[vmem() for _ in out_shape] if many else vmem(),
        compiler_params=pltpu.CompilerParams(vmem_limit_bytes=32 * 1024 * 1024),
    )


def head_columns(columns):
    lane = lax.broadcasted_iota(jnp.int32, (ROWS, CHANNELS), 1) // WIDTH
    wide = jnp.broadcast_to(columns[0], (ROWS, CHANNELS))
    for h in range(1, HEADS):
        wide = jnp.where(lane == h, columns[h], wide)
    return wide


def scan_kernel(place, seg, step_raw, decay_log, skip, x_ref, b_ref, c_ref, inner, carry, msg):
    row_start = place[0] * ROWS
    boundary = seg.shape[0] * seg.shape[1] - jnp.sum(seg[...])
    raw = step_raw[...]
    step = jnp.maximum(raw, 0.0) + jnp.log1p(jnp.exp(-jnp.abs(raw)))
    log_decay = -jnp.exp(decay_log[...]) * step
    share = ROWS // HEADS
    lane = lax.broadcasted_iota(jnp.int32, (ROWS, ROWS), 1)
    row = lax.broadcasted_iota(jnp.int32, (ROWS, ROWS), 0)
    spread = jnp.broadcast_to(log_decay[:, 0:1], (ROWS, ROWS))
    for h in range(1, HEADS):
        spread = jnp.where(lane // share == h, log_decay[:, h : h + 1], spread)
    below = (row >= lane).astype(F32)
    total = dot(below, spread, HIGH)
    total_t = total.T
    columns = [total[:, share * h : share * h + 1] for h in range(HEADS)]
    wide = head_columns(columns)
    places = row_start + lax.broadcasted_iota(jnp.int32, (ROWS, 1), 0)
    seg_rows = (places >= boundary).astype(jnp.int32)
    seg_lanes = (row_start + lane >= boundary).astype(jnp.int32)
    seg_before = (jnp.maximum(row_start - 1, 0) >= boundary).astype(jnp.int32)
    seg_last = (row_start + ROWS - 1 >= boundary).astype(jnp.int32)
    allowed = (row >= lane) & (seg_rows == seg_lanes)
    inputs = x_ref[...].astype(F32)
    scaled = head_columns([step[:, h : h + 1] for h in range(HEADS)]) * inputs
    scores = lax.dot_general(
        c_ref[...], b_ref[...], (((1,), (1,)), ((), ())), preferred_element_type=F32
    )
    for h in range(HEADS):
        gap = columns[h] - total_t[share * h : share * h + 1, :]
        weight = jnp.where(allowed, jnp.exp(jnp.where(allowed, gap, 0.0)), 0.0)
        part = slice(h * WIDTH, (h + 1) * WIDTH)
        inner[:, part] = dot(scores * weight, scaled[:, part], HIGH)
    inner[...] += skip[...] * inputs
    carry[...] = jnp.where(seg_rows == seg_before, jnp.exp(wide), 0.0)
    last = wide[ROWS - 1 : ROWS, :]
    to_end = jnp.where(seg_rows == seg_last, jnp.exp(last - wide), 0.0)
    msg[0:STATE, :] = lax.dot_general(
        b_ref[...].astype(F32),
        scaled * to_end,
        (((0,), (0,)), ((), ())),
        preferred_element_type=F32,
        precision=HIGH,
    )
    keep = jnp.where(seg_last == seg_before, jnp.exp(last), 0.0)
    msg[STATE : STATE + 8, :] = jnp.broadcast_to(keep, (8, CHANNELS))


def chip_kernel(pair, out):
    keep = [pair[k, STATE : STATE + 1, :] for k in range(NC)]
    out[0:STATE, :] = (keep[1] * pair[0, 0:STATE, :] + pair[1, 0:STATE, :]).astype(BF16)
    both = keep[0] * keep[1]
    coarse = both.astype(BF16).astype(F32)
    line = lax.broadcasted_iota(jnp.int32, (MSG - STATE, CHANNELS), 0)
    out[STATE:MSG, :] = jnp.where(line == 0, coarse, jnp.where(line == 1, both - coarse, 0.0)).astype(
        BF16
    )


def gate_kernel(place, chips, pair, c_ref, inner, carry, gate, out, squares):
    y, core = (place[1], place[2])
    state = jnp.zeros((STATE, CHANNELS), F32)
    for k in range(NY - 1):
        tail = chips[k, STATE:MSG, :].astype(F32)
        keep = tail[0:1, :] + tail[1:2, :]
        state = jnp.where(k < y, keep * state + chips[k, 0:STATE, :].astype(F32), state)
    state = jnp.where(
        core == 1, pair[0, STATE : STATE + 1, :] * state + pair[0, 0:STATE, :], state
    )
    ssd = inner[...] + carry[...] * dot(c_ref[...].astype(F32), state, HIGH)
    v = gate[...].astype(F32)
    gated = (ssd * (v / (1.0 + jnp.exp(-v)))).astype(BF16)
    out[...] = gated
    rounded = gated.astype(F32)
    column = jnp.sum(rounded * rounded, axis=1, keepdims=True)
    squares[...] = jnp.broadcast_to(column, (ROWS, ROWS)).T[0:8, :]


def norm_kernel(place, gated, squares, gain, out):
    line = jnp.sum(squares[...], axis=0, keepdims=True)
    scale = lax.rsqrt(jnp.broadcast_to(line, (ROWS, ROWS)).T / 2048.0 + EPS)
    wide = jnp.concatenate([scale] * (CHANNELS // ROWS), axis=1)
    out[...] = (gated[...].astype(F32) * wide * gain[pl.ds(place[5], 1), :]).astype(BF16)


def project_kernel(other, place, rows, weight, *rest):
    before, out = rest if other else (None,) + rest
    side = lax.rem(place[6] + other, NL)
    total = before[...] if other else jnp.zeros((ROWS, NX * ROWS), F32)
    for g in range(NG):
        total = total + dot(
            rows[g], jnp.concatenate([weight[g, k, side] for k in range(NX)], axis=1)
        )
    if other:
        for k in range(NX):
            out[k] = total[:, k * ROWS : (k + 1) * ROWS]
    else:
        out[...] = total


def project(place, rows, weight, before=None):
    other = 0 if before is None else 1
    return pl.pallas_call(
        lambda *refs: project_kernel(other, *refs),
        out_shape=jax.ShapeDtypeStruct((NX, ROWS, ROWS) if other else (ROWS, NX * ROWS), F32),
        in_specs=[smem()] + [vmem()] * (2 + other),
        out_specs=vmem(),
        cost_estimate=pl.CostEstimate(
            flops=2 * ROWS * NG * CHANNELS * NX * ROWS, bytes_accessed=1 << 22, transcendentals=0
        ),
        compiler_params=pltpu.CompilerParams(vmem_limit_bytes=32 * 1024 * 1024),
    )(place, rows, weight, *([before] if other else []))


def residual_kernel(parts, residual, mixer_out, summed):
    mixed = ((parts[0] + parts[1]) + (parts[2] + parts[3])).astype(BF16)
    mixer_out[...] = mixed
    summed[...] = (residual[...].astype(F32) + mixed.astype(F32)).astype(BF16)


def head_kernel(place, p0, p1, p2, p3, gain, wanted, weight, out, total, squares):
    s = pl.program_id(0)

    @pl.when(s == 0)
    def _():
        total[...] = jnp.zeros_like(total)
        squares[...] = jnp.zeros_like(squares)

    square = jnp.zeros((ROWS, ROWS), F32)
    result = total[...]
    for k, part in enumerate((p0, p1, p2, p3)):
        source = lax.rem(place[4] + NX - k, NX)
        blocks = []
        for half in range(NL):
            v = part[half].astype(F32)
            square = square + v * v
            blocks.append((v * gain[half, source]).astype(BF16))
        pieces = [weight[0, half, source] for half in range(NL)]
        result = result + dot(
            jnp.concatenate(blocks, axis=1), jnp.concatenate(pieces, axis=0)
        )
    total[...] = result
    squares[...] += square

    @pl.when(s == pl.num_programs(0) - 1)
    def _():
        mean = jnp.sum(squares[...], axis=1, keepdims=True) / 8192.0
        logits = total[...] * lax.rsqrt(mean + EPS)
        top = jnp.max(logits, axis=1, keepdims=True)
        mass = jnp.sum(jnp.exp(logits - top), axis=1, keepdims=True)
        first = place[5] * logits.shape[1]
        vocab = first + lax.broadcasted_iota(jnp.int32, logits.shape, 1)
        picked = jnp.sum(jnp.where(vocab == wanted[...], logits, 0.0), axis=1, keepdims=True)
        lane = lax.broadcasted_iota(jnp.int32, (ROWS, ROWS), 1)
        out[...] = jnp.where(lane % 2 == 0, top + jnp.log(mass), picked).T


def head(place, parts, gain, wanted, weight):
    columns = weight.shape[-1]
    return pl.pallas_call(
        head_kernel,
        grid=(NG,),
        out_shape=jax.ShapeDtypeStruct((ROWS, ROWS), F32),
        in_specs=[smem()]
        + [pl.BlockSpec((NL, ROWS, ROWS), lambda s: (s, 0, 0))] * NX
        + [
            pl.BlockSpec((NL, NX, 1, ROWS), lambda s: (s, 0, 0, 0)),
            pl.BlockSpec((ROWS, 1), lambda s: (0, 0)),
            pl.BlockSpec((1, NL, NX, ROWS, columns), lambda s: (s, 0, 0, 0, 0)),
        ],
        out_specs=pl.BlockSpec((ROWS, ROWS), lambda s: (0, 0)),
        scratch_shapes=[pltpu.VMEM((ROWS, columns), F32), pltpu.VMEM((ROWS, ROWS), F32)],
        cost_estimate=pl.CostEstimate(
            flops=2 * ROWS * NX * NZ * ROWS * columns, bytes_accessed=18 << 20, transcendentals=0
        ),
        compiler_params=pltpu.CompilerParams(vmem_limit_bytes=52 * 1024 * 1024),
    )(place, *parts, gain, wanted, weight)


def token_kernel(place, stats, seg, mask, logp, sums):
    even = lax.broadcasted_iota(jnp.int32, (ROWS, ROWS), 0) % 2 == 0
    table = stats[...]
    least = jnp.where(even, table, -jnp.inf)
    top = jnp.max(least, axis=0, keepdims=True)
    mass = jnp.sum(jnp.where(even, jnp.exp(least - top), 0.0), axis=0, keepdims=True)
    picked = jnp.sum(jnp.where(even, 0.0, table), axis=0, keepdims=True)
    value = picked - (top + jnp.log(mass))
    logp[...] = value
    mine = pl.ds(place[0], 1)
    counted = mask[mine, :] == 1
    lane = lax.broadcasted_iota(jnp.int32, (8, ROWS), 1)
    both = jnp.zeros((8, ROWS), F32)
    for k in range(2):
        chosen = jnp.where(counted & (seg[mine, :] == k), value, 0.0)
        both = jnp.where(lane == k, jnp.sum(chosen, axis=1, keepdims=True), both)
    sums[...] = both


def mean_kernel(sums, seg, mask, out):
    every = jnp.sum(sums[...], axis=0, keepdims=True)
    means = []
    for k in range(2):
        count = jnp.sum(jnp.where((mask[...] == 1) & (seg[...] == k), 1.0, 0.0))
        means.append(every[:, k : k + 1] / count)
    lane = lax.broadcasted_iota(jnp.int32, (1, ROWS), 1)
    out[...] = jnp.where(
        lane == 0, means[0], jnp.where(lane == 1, means[1], means[0] - means[1])
    )


def shifted(part, axis, k):
    n = lax.axis_size(axis)
    return lax.ppermute(part, axis, [(i, (i + k) % n) for i in range(n)])


def local(
    residual_in,
    ssm_input,
    gate_input,
    b_proj,
    c_proj,
    step_raw,
    decay_log,
    skip_gain,
    mixer_gain,
    out_weight,
    final_gain,
    head_weight,
    targets,
    segment_ids,
    loss_mask,
):
    y, core, zl, x = [lax.axis_index(axis) for axis in ("y", "core", "zl", "x")]
    group = lax.axis_index("zg")
    z = group * NL + zl
    seq = y * NC + core
    place = jnp.stack([seq, y, core, z, x, z * NX + x, zl]).astype(jnp.int32)
    seg = segment_ids.reshape(-1, ROWS)
    mask = loss_mask.reshape(-1, ROWS)
    b_rows = lax.dynamic_index_in_dim(b_proj, group, 1, keepdims=False)
    c_rows = lax.dynamic_index_in_dim(c_proj, group, 1, keepdims=False)

    inner, carry, msg = call(
        scan_kernel,
        (
            jax.ShapeDtypeStruct((ROWS, CHANNELS), F32),
            jax.ShapeDtypeStruct((ROWS, CHANNELS), F32),
            jax.ShapeDtypeStruct((STATE + 8, CHANNELS), F32),
        ),
        [smem()] + [vmem()] * 7,
    )(
        place,
        seg,
        step_raw,
        decay_log.reshape(1, HEADS),
        jnp.repeat(skip_gain, WIDTH).reshape(1, CHANNELS),
        ssm_input,
        b_rows,
        c_rows,
    )
    turned = lax.all_to_all(out_weight.reshape(NL, NX, CHANNELS, ROWS), "x", 1, 0)
    out_rows = lax.all_gather(turned, SEQ)
    head_rows = lax.all_gather(head_weight, SEQ)

    pair = lax.all_gather(msg, "core")
    chip = call(chip_kernel, jax.ShapeDtypeStruct((MSG, CHANNELS), BF16), [vmem()])(pair)
    chips = lax.all_gather(chip, "y")
    gated, squares = call(
        gate_kernel,
        (
            jax.ShapeDtypeStruct((ROWS, CHANNELS), BF16),
            jax.ShapeDtypeStruct((8, ROWS), F32),
        ),
        [smem()] + [vmem()] * 6,
    )(place, chips, pair, c_rows, inner, carry, gate_input)
    squares = lax.all_to_all(squares, ("zl", "x"), 0, 0, tiled=True)
    normed = call(
        norm_kernel, jax.ShapeDtypeStruct((ROWS, CHANNELS), BF16), [smem()] + [vmem()] * 3
    )(place, gated, squares, mixer_gain.reshape(-1, CHANNELS))
    same = lax.all_gather(normed, "zg")
    other = shifted(same, "zl", 1)
    total = project(place, same, out_rows)
    parts = lax.all_to_all(project(place, other, out_rows, total), "x", 0, 0)
    half = jax.ShapeDtypeStruct((ROWS, ROWS), BF16)
    mixer_out, summed = call(residual_kernel, (half, half), [vmem()] * 2)(parts, residual_in)

    column = lax.all_gather(summed, ("zg", "zl"))
    features = [column] + [shifted(column, "x", k) for k in range(1, NX)]
    wanted = lax.dynamic_slice_in_dim(targets, seq * ROWS, ROWS).reshape(ROWS, 1)
    gains = final_gain.reshape(NZ, NX, 1, ROWS)
    matrix = head_rows.reshape(NG, NL, NX, ROWS, -1)
    stats = head(place, features, gains, wanted, matrix)
    stats = lax.all_to_all(stats, MP, 0, 0, tiled=True)
    logp, sums = call(
        token_kernel,
        (jax.ShapeDtypeStruct((1, ROWS), F32), jax.ShapeDtypeStruct((8, ROWS), F32)),
        [smem()] + [vmem()] * 3,
    )(place, stats, seg, mask)
    sums = lax.all_to_all(sums, SEQ, 0, 0, tiled=True)
    means = call(mean_kernel, jax.ShapeDtypeStruct((1, ROWS), F32), [vmem()] * 3)(sums, seg, mask)
    return (mixer_out, logp.reshape(ROWS), means[0, :3])


def solution(mesh):
    fine = Mesh(mesh.devices.reshape(NY, NC, NG, NL, NX), AXES)
    mp = MP
    in_specs = (
        P(SEQ, mp),
        P(SEQ, mp),
        P(SEQ, mp),
        P(SEQ, None, None),
        P(SEQ, None, None),
        P(SEQ, mp),
        P(mp),
        P(mp),
        P(),
        P(SEQ, mp),
        P(),
        P(SEQ, mp),
        P(),
        P(),
        P(),
    )
    out_specs = (P(SEQ, mp), P(SEQ), P())
    return jax.shard_map(local, mesh=fine, in_specs=in_specs, out_specs=out_specs, check_vma=False)
```

```python
import jax
import jax.numpy as jnp
from jax import lax
from jax.experimental import pallas as pl
from jax.experimental.pallas import tpu as pltpu
from jax.sharding import Mesh, PartitionSpec as P

EPS = 1e-05
HIGH = lax.Precision.HIGHEST
F32 = jnp.float32
BF16 = jnp.bfloat16

NY, NC, NG, NL, NX = (4, 2, 8, 2, 4)
NZ = NG * NL
AXES = ("y", "core", "zg", "zl", "x")
SEQ = ("y", "core")
MP = ("zg", "zl", "x")
ROWS = 128
HEADS = 4
WIDTH = 64
CHANNELS = HEADS * WIDTH
STATE = 256
GROUPS = 8
MSG = STATE + 16


def dot(a, b, precision=None):
    return jnp.dot(a, b, preferred_element_type=F32, precision=precision)


def vmem():
    return pl.BlockSpec(memory_space=pltpu.VMEM)


def smem():
    return pl.BlockSpec(memory_space=pltpu.SMEM)


def call(body, out_shape, specs):
    many = isinstance(out_shape, (tuple, list))
    return pl.pallas_call(
        body,
        out_shape=out_shape,
        in_specs=specs,
        out_specs=[vmem() for _ in out_shape] if many else vmem(),
        compiler_params=pltpu.CompilerParams(vmem_limit_bytes=32 * 1024 * 1024),
    )


def head_columns(columns):
    lane = lax.broadcasted_iota(jnp.int32, (ROWS, CHANNELS), 1) // WIDTH
    wide = jnp.broadcast_to(columns[0], (ROWS, CHANNELS))
    for h in range(1, HEADS):
        wide = jnp.where(lane == h, columns[h], wide)
    return wide


def scan_kernel(place, seg, step_raw, decay_log, skip, x_ref, b_ref, c_ref, inner, carry, msg):
    row_start = place[0] * ROWS
    boundary = seg.shape[0] * seg.shape[1] - jnp.sum(seg[...])
    raw = jnp.concatenate([step_raw[...]] * (ROWS // HEADS), axis=0).T[:, 0:HEADS]
    step = jnp.maximum(raw, 0.0) + jnp.log1p(jnp.exp(-jnp.abs(raw)))
    log_decay = -jnp.exp(decay_log[...]) * step
    share = ROWS // HEADS
    lane = lax.broadcasted_iota(jnp.int32, (ROWS, ROWS), 1)
    row = lax.broadcasted_iota(jnp.int32, (ROWS, ROWS), 0)
    spread = jnp.broadcast_to(log_decay[:, 0:1], (ROWS, ROWS))
    for h in range(1, HEADS):
        spread = jnp.where(lane // share == h, log_decay[:, h : h + 1], spread)
    below = (row >= lane).astype(F32)
    total = dot(below, spread, HIGH)
    total_t = total.T
    columns = [total[:, share * h : share * h + 1] for h in range(HEADS)]
    wide = head_columns(columns)
    places = row_start + lax.broadcasted_iota(jnp.int32, (ROWS, 1), 0)
    seg_rows = (places >= boundary).astype(jnp.int32)
    seg_lanes = (row_start + lane >= boundary).astype(jnp.int32)
    seg_before = (jnp.maximum(row_start - 1, 0) >= boundary).astype(jnp.int32)
    seg_last = (row_start + ROWS - 1 >= boundary).astype(jnp.int32)
    allowed = (row >= lane) & (seg_rows == seg_lanes)
    inputs = x_ref[...].astype(F32)
    scaled = head_columns([step[:, h : h + 1] for h in range(HEADS)]) * inputs
    scores = lax.dot_general(
        c_ref[...], b_ref[...], (((1,), (1,)), ((), ())), preferred_element_type=F32
    )
    for h in range(HEADS):
        gap = columns[h] - total_t[share * h : share * h + 1, :]
        weight = jnp.where(allowed, jnp.exp(jnp.where(allowed, gap, 0.0)), 0.0)
        part = slice(h * WIDTH, (h + 1) * WIDTH)
        inner[:, part] = dot(scores * weight, scaled[:, part], HIGH)
    gains = jnp.broadcast_to(skip[...], (ROWS, HEADS))
    inner[...] += head_columns([gains[:, h : h + 1] for h in range(HEADS)]) * inputs
    carry[...] = jnp.where(seg_rows == seg_before, jnp.exp(wide), 0.0)
    last = wide[ROWS - 1 : ROWS, :]
    to_end = jnp.where(seg_rows == seg_last, jnp.exp(last - wide), 0.0)
    msg[0:STATE, :] = lax.dot_general(
        b_ref[...].astype(F32),
        scaled * to_end,
        (((0,), (0,)), ((), ())),
        preferred_element_type=F32,
        precision=HIGH,
    )
    keep = jnp.where(seg_last == seg_before, jnp.exp(last), 0.0)
    msg[STATE : STATE + 8, :] = jnp.broadcast_to(keep, (8, CHANNELS))


def chip_kernel(pair, out):
    keep = [pair[k, STATE : STATE + 1, :] for k in range(NC)]
    out[0:STATE, :] = (keep[1] * pair[0, 0:STATE, :] + pair[1, 0:STATE, :]).astype(BF16)
    both = keep[0] * keep[1]
    coarse = both.astype(BF16).astype(F32)
    line = lax.broadcasted_iota(jnp.int32, (MSG - STATE, CHANNELS), 0)
    out[STATE:MSG, :] = jnp.where(line == 0, coarse, jnp.where(line == 1, both - coarse, 0.0)).astype(
        BF16
    )


def gate_kernel(place, chips, pair, c_ref, inner, carry, gate, out):
    y, core = (place[1], place[2])
    state = jnp.zeros((STATE, CHANNELS), F32)
    for k in range(NY - 1):
        tail = chips[k, STATE:MSG, :].astype(F32)
        keep = tail[0:1, :] + tail[1:2, :]
        state = jnp.where(k < y, keep * state + chips[k, 0:STATE, :].astype(F32), state)
    state = jnp.where(
        core == 1, pair[0, STATE : STATE + 1, :] * state + pair[0, 0:STATE, :], state
    )
    ssd = inner[...] + carry[...] * dot(c_ref[...].astype(F32), state, HIGH)
    v = gate[...].astype(F32)
    out[...] = (ssd * (v / (1.0 + jnp.exp(-v)))).astype(BF16)


def square_kernel(rows, out):
    lane = lax.broadcasted_iota(jnp.int32, (ROWS, ROWS), 1)
    table = jnp.zeros((ROWS, ROWS), F32)
    for g in range(NG):
        v = rows[g].astype(F32)
        table = jnp.where(lane == g, jnp.sum(v * v, axis=1, keepdims=True), table)
    line = table.T[0:NG, :]
    for k in range(NL * NX):
        out[k] = line


def project_kernel(place, mine, paired, squares, gain, same, other, out):
    side = place[6]
    total = squares[0]
    for k in range(1, NL * NX):
        total = total + squares[k]
    scale = lax.rsqrt(total / 2048.0 + EPS)
    scale = jnp.concatenate([scale] * (ROWS // NG), axis=0).T
    result = jnp.zeros((ROWS, NX * ROWS), F32)
    lane = lax.broadcasted_iota(jnp.int32, (ROWS, ROWS), 1)
    for c, weight in enumerate((same, other)):
        core = lax.rem(place[2] + c, NC)
        for j in range(NY):
            g = j * NC + core
            column = jnp.sum(jnp.where(lane == g, scale, 0.0), axis=1, keepdims=True)
            for rows, half in ((mine, side), (paired, 1 - side)):
                line = (NL * g + half) * NX + place[4]
                normed = (rows[g].astype(F32) * column * gain[pl.ds(line, 1), :]).astype(BF16)
                block = jnp.concatenate([weight[j, k, half] for k in range(NX)], axis=1)
                result = result + dot(normed, block)
    for k in range(NX):
        out[k] = result[:, k * ROWS : (k + 1) * ROWS]


def residual_kernel(parts, residual, mixer_out, summed):
    mixed = ((parts[0] + parts[1]) + (parts[2] + parts[3])).astype(BF16)
    mixer_out[...] = mixed
    summed[...] = (residual[...].astype(F32) + mixed.astype(F32)).astype(BF16)


def scaled_blocks(parts, sources, gain, g, square):
    blocks = []
    for part, source in zip(parts, sources):
        for half in range(NL):
            v = part[NL * g + half].astype(F32)
            square = square + v * v
            blocks.append((v * gain[NL * g + half, source]).astype(BF16))
    return jnp.concatenate(blocks, axis=1), square


def own_kernel(place, part, gain, weight, total, squares, later, held, arrived):
    copies = []
    for k in range(NX):
        source = lax.rem(place[4] + NX - k, NX)
        for g in range(NG):
            for half in range(NL):
                target = later.at[g, k - 1, half] if k else held.at[g, half]
                copies.append(
                    pltpu.make_async_copy(
                        weight.at[g, half, source], target, arrived.at[k, g, half]
                    )
                )
                copies[-1].start()
    result = jnp.zeros(total.shape, F32)
    square = jnp.zeros(squares.shape, F32)
    for g in range(NG):
        rows, square = scaled_blocks([part], [place[4]], gain, g, square)
        for half in range(NL):
            copies[NL * g + half].wait()
        result = result + dot(rows, jnp.concatenate([held[g, h] for h in range(NL)], axis=0))
    total[...] = result
    squares[...] = square
    for copy in copies[NG * NL :]:
        copy.wait()


def rest_kernel(place, p1, p2, p3, gain, weight, total, squares, wanted, out):
    parts = (p1, p2, p3)
    sources = [lax.rem(place[4] + NX - k, NX) for k in range(1, NX)]
    result = total[...]
    square = squares[...]
    for g in range(NG):
        rows, square = scaled_blocks(parts, sources, gain, g, square)
        pieces = [weight[g, k, half] for k in range(NX - 1) for half in range(NL)]
        result = result + dot(rows, jnp.concatenate(pieces, axis=0))
    mean = jnp.sum(square, axis=1, keepdims=True) / 8192.0
    logits = result * lax.rsqrt(mean + EPS)
    top = jnp.max(logits, axis=1, keepdims=True)
    mass = jnp.sum(jnp.exp(logits - top), axis=1, keepdims=True)
    begin = place[5] * logits.shape[1]
    vocab = begin + lax.broadcasted_iota(jnp.int32, logits.shape, 1)
    picked = jnp.sum(jnp.where(vocab == wanted[...], logits, 0.0), axis=1, keepdims=True)
    lane = lax.broadcasted_iota(jnp.int32, (ROWS, ROWS), 1)
    out[...] = jnp.where(lane % 2 == 0, top + jnp.log(mass), picked).T


def head(place, parts, gain, weight, wanted):
    columns = weight.shape[-1]
    square = jax.ShapeDtypeStruct((ROWS, ROWS), F32)
    cost = pl.CostEstimate(
        flops=2 * ROWS * NZ * ROWS * columns, bytes_accessed=1 << 24, transcendentals=0
    )
    params = pltpu.CompilerParams(vmem_limit_bytes=32 * 1024 * 1024)
    total, squares, later = pl.pallas_call(
        own_kernel,
        out_shape=(
            jax.ShapeDtypeStruct((ROWS, columns), F32),
            square,
            jax.ShapeDtypeStruct((NG, NX - 1, NL, ROWS, columns), BF16),
        ),
        in_specs=[smem(), vmem(), vmem(), pl.BlockSpec(memory_space=pl.ANY)],
        out_specs=[vmem()] * 3,
        scratch_shapes=[
            pltpu.VMEM((NG, NL, ROWS, columns), BF16),
            pltpu.SemaphoreType.DMA((NX, NG, NL)),
        ],
        cost_estimate=cost,
        compiler_params=params,
    )(place, parts[0], gain, weight)
    return pl.pallas_call(
        rest_kernel,
        out_shape=square,
        in_specs=[smem()] + [vmem()] * (NX + 4),
        out_specs=vmem(),
        cost_estimate=cost,
        compiler_params=params,
    )(place, *parts[1:], gain, later, total, squares, wanted)


def token_kernel(place, stats, seg, mask, logp, sums):
    even = lax.broadcasted_iota(jnp.int32, (ROWS, ROWS), 0) % 2 == 0
    table = stats[...]
    least = jnp.where(even, table, -jnp.inf)
    top = jnp.max(least, axis=0, keepdims=True)
    mass = jnp.sum(jnp.where(even, jnp.exp(least - top), 0.0), axis=0, keepdims=True)
    picked = jnp.sum(jnp.where(even, 0.0, table), axis=0, keepdims=True)
    value = picked - (top + jnp.log(mass))
    logp[...] = value
    mine = pl.ds(place[0], 1)
    counted = mask[mine, :] == 1
    lane = lax.broadcasted_iota(jnp.int32, (8, ROWS), 1)
    both = jnp.zeros((8, ROWS), F32)
    for k in range(2):
        chosen = jnp.where(counted & (seg[mine, :] == k), value, 0.0)
        both = jnp.where(lane == k, jnp.sum(chosen, axis=1, keepdims=True), both)
    sums[...] = both


def mean_kernel(sums, seg, mask, out):
    every = jnp.sum(sums[...], axis=0, keepdims=True)
    means = []
    for k in range(2):
        count = jnp.sum(jnp.where((mask[...] == 1) & (seg[...] == k), 1.0, 0.0))
        means.append(every[:, k : k + 1] / count)
    lane = lax.broadcasted_iota(jnp.int32, (1, ROWS), 1)
    out[...] = jnp.where(
        lane == 0, means[0], jnp.where(lane == 1, means[1], means[0] - means[1])
    )


def shifted(part, axis, k):
    n = lax.axis_size(axis)
    return lax.ppermute(part, axis, [(i, (i + k) % n) for i in range(n)])


def local(
    residual_in,
    ssm_input,
    gate_input,
    b_proj,
    c_proj,
    step_raw,
    decay_log,
    skip_gain,
    mixer_gain,
    out_weight,
    final_gain,
    head_weight,
    targets,
    segment_ids,
    loss_mask,
):
    y, core, zl, x = [lax.axis_index(axis) for axis in ("y", "core", "zl", "x")]
    group = lax.axis_index("zg")
    z = group * NL + zl
    seq = y * NC + core
    place = jnp.stack([seq, y, core, z, x, z * NX + x, zl]).astype(jnp.int32)
    seg = segment_ids.reshape(-1, ROWS)
    mask = loss_mask.reshape(-1, ROWS)
    b_rows = lax.dynamic_index_in_dim(b_proj, group, 1, keepdims=False)
    c_rows = lax.dynamic_index_in_dim(c_proj, group, 1, keepdims=False)

    rows = out_weight.reshape(1, NL, NX, CHANNELS, ROWS).transpose(0, 2, 1, 3, 4)
    rows = jnp.broadcast_to(rows, (NY, *rows.shape[1:])).reshape(NY * NX, NL, CHANNELS, ROWS)
    rows, b_rows = lax.optimization_barrier((rows, b_rows))
    inner, carry, msg = call(
        scan_kernel,
        (
            jax.ShapeDtypeStruct((ROWS, CHANNELS), F32),
            jax.ShapeDtypeStruct((ROWS, CHANNELS), F32),
            jax.ShapeDtypeStruct((STATE + 8, CHANNELS), F32),
        ),
        [smem()] + [vmem()] * 7,
    )(
        place,
        seg,
        step_raw.T,
        decay_log.reshape(1, HEADS),
        skip_gain.reshape(1, HEADS),
        ssm_input,
        b_rows,
        c_rows,
    )
    pair = lax.all_gather(msg, "core")
    chip = call(chip_kernel, jax.ShapeDtypeStruct((MSG, CHANNELS), BF16), [vmem()])(pair)
    chips = lax.all_gather(chip, "y")
    gated = call(
        gate_kernel, jax.ShapeDtypeStruct((ROWS, CHANNELS), BF16), [smem()] + [vmem()] * 6
    )(place, chips, pair, c_rows, inner, carry, gate_input)
    rows, weight, gated = lax.optimization_barrier((rows, head_weight, gated))
    same = lax.all_to_all(rows, ("y", "x"), 0, 0).reshape(NY, NX, NL, CHANNELS, ROWS)
    head_rows = lax.all_gather(weight, SEQ)
    mine = lax.all_gather(gated, "zg")
    odd = range(1, NZ, NL)
    swaps = [(i, (i + 1) % NZ) for i in odd] + [((i + 1) % NZ, i) for i in odd]
    same, mine = lax.optimization_barrier((same, mine))
    other = shifted(same, "core", 1)
    paired = lax.ppermute(mine, ("zg", "zl"), swaps)
    squares = call(
        square_kernel, jax.ShapeDtypeStruct((NL * NX, NG, ROWS), F32), [vmem()]
    )(mine)
    squares = lax.all_to_all(squares, ("zl", "x"), 0, 0)
    parts = call(
        project_kernel, jax.ShapeDtypeStruct((NX, ROWS, ROWS), F32), [smem()] + [vmem()] * 6
    )(place, mine, paired, squares, mixer_gain.reshape(-1, CHANNELS), same, other)
    parts = lax.all_to_all(parts, "x", 0, 0)
    half = jax.ShapeDtypeStruct((ROWS, ROWS), BF16)
    mixer_out, summed = call(residual_kernel, (half, half), [vmem()] * 2)(parts, residual_in)

    column = lax.all_gather(summed, ("zg", "zl"))
    features = [column] + [shifted(column, "x", k) for k in range(1, NX)]
    wanted = lax.dynamic_slice_in_dim(targets, seq * ROWS, ROWS).reshape(ROWS, 1)
    gains = final_gain.reshape(NZ, NX, 1, ROWS)
    matrix = head_rows.reshape(NG, NL, NX, ROWS, -1)
    stats = head(place, features, gains, matrix, wanted)
    stats = lax.all_to_all(stats, MP, 0, 0, tiled=True)
    logp, sums = call(
        token_kernel,
        (jax.ShapeDtypeStruct((1, ROWS), F32), jax.ShapeDtypeStruct((8, ROWS), F32)),
        [smem()] + [vmem()] * 3,
    )(place, stats, seg, mask)
    sums = lax.all_to_all(sums, SEQ, 0, 0, tiled=True)
    means = call(mean_kernel, jax.ShapeDtypeStruct((1, ROWS), F32), [vmem()] * 3)(sums, seg, mask)
    return (mixer_out, logp.reshape(ROWS), means[0, :3])


def solution(mesh):
    fine = Mesh(mesh.devices.reshape(NY, NC, NG, NL, NX), AXES)
    mp = MP
    in_specs = (
        P(SEQ, mp),
        P(SEQ, mp),
        P(SEQ, mp),
        P(SEQ, None, None),
        P(SEQ, None, None),
        P(SEQ, mp),
        P(mp),
        P(mp),
        P(),
        P(SEQ, mp),
        P(),
        P(SEQ, mp),
        P(),
        P(),
        P(),
    )
    out_specs = (P(SEQ, mp), P(SEQ), P())
    return jax.shard_map(local, mesh=fine, in_specs=in_specs, out_specs=out_specs, check_vma=False)
```

```python
import jax
import jax.numpy as jnp
from jax import lax
from jax.experimental import pallas as pl
from jax.experimental.pallas import tpu as pltpu
from jax.sharding import Mesh, PartitionSpec as P

EPS = 1e-05
HIGH = lax.Precision.HIGHEST
F32 = jnp.float32
BF16 = jnp.bfloat16

NY, NC, NG, NL, NX = (4, 2, 8, 2, 4)
NZ = NG * NL
AXES = ("y", "core", "zg", "zl", "x")
SEQ = ("y", "core")
MP = ("zg", "zl", "x")
ROWS = 128
HEADS = 4
WIDTH = 64
CHANNELS = HEADS * WIDTH
STATE = 256
GROUPS = 8
MSG = STATE + 16


def dot(a, b, precision=None):
    return jnp.dot(a, b, preferred_element_type=F32, precision=precision)


def vmem():
    return pl.BlockSpec(memory_space=pltpu.VMEM)


def smem():
    return pl.BlockSpec(memory_space=pltpu.SMEM)


def call(body, out_shape, specs):
    many = isinstance(out_shape, (tuple, list))
    return pl.pallas_call(
        body,
        out_shape=out_shape,
        in_specs=specs,
        out_specs=[vmem() for _ in out_shape] if many else vmem(),
        compiler_params=pltpu.CompilerParams(vmem_limit_bytes=32 * 1024 * 1024),
    )


def head_columns(columns):
    lane = lax.broadcasted_iota(jnp.int32, (ROWS, CHANNELS), 1) // WIDTH
    wide = jnp.broadcast_to(columns[0], (ROWS, CHANNELS))
    for h in range(1, HEADS):
        wide = jnp.where(lane == h, columns[h], wide)
    return wide


def scan_kernel(place, seg, step_raw, decay_log, skip, x_ref, b_ref, c_ref, inner, carry, msg):
    row_start = place[0] * ROWS
    boundary = seg.shape[0] * seg.shape[1] - jnp.sum(seg[...])
    raw = jnp.concatenate([step_raw[...]] * (ROWS // HEADS), axis=0).T[:, 0:HEADS]
    step = jnp.maximum(raw, 0.0) + jnp.log1p(jnp.exp(-jnp.abs(raw)))
    log_decay = -jnp.exp(decay_log[...]) * step
    share = ROWS // HEADS
    lane = lax.broadcasted_iota(jnp.int32, (ROWS, ROWS), 1)
    row = lax.broadcasted_iota(jnp.int32, (ROWS, ROWS), 0)
    spread = jnp.broadcast_to(log_decay[:, 0:1], (ROWS, ROWS))
    for h in range(1, HEADS):
        spread = jnp.where(lane // share == h, log_decay[:, h : h + 1], spread)
    below = (row >= lane).astype(F32)
    total = dot(below, spread, HIGH)
    total_t = total.T
    columns = [total[:, share * h : share * h + 1] for h in range(HEADS)]
    wide = head_columns(columns)
    places = row_start + lax.broadcasted_iota(jnp.int32, (ROWS, 1), 0)
    seg_rows = (places >= boundary).astype(jnp.int32)
    seg_lanes = (row_start + lane >= boundary).astype(jnp.int32)
    seg_before = (jnp.maximum(row_start - 1, 0) >= boundary).astype(jnp.int32)
    seg_last = (row_start + ROWS - 1 >= boundary).astype(jnp.int32)
    allowed = (row >= lane) & (seg_rows == seg_lanes)
    inputs = x_ref[...].astype(F32)
    scaled = head_columns([step[:, h : h + 1] for h in range(HEADS)]) * inputs
    scores = lax.dot_general(
        c_ref[...], b_ref[...], (((1,), (1,)), ((), ())), preferred_element_type=F32
    )
    for h in range(HEADS):
        gap = columns[h] - total_t[share * h : share * h + 1, :]
        weight = jnp.where(allowed, jnp.exp(jnp.where(allowed, gap, 0.0)), 0.0)
        part = slice(h * WIDTH, (h + 1) * WIDTH)
        inner[:, part] = dot(scores * weight, scaled[:, part], HIGH)
    gains = jnp.broadcast_to(skip[...], (ROWS, HEADS))
    inner[...] += head_columns([gains[:, h : h + 1] for h in range(HEADS)]) * inputs
    carry[...] = jnp.where(seg_rows == seg_before, jnp.exp(wide), 0.0)
    last = wide[ROWS - 1 : ROWS, :]
    to_end = jnp.where(seg_rows == seg_last, jnp.exp(last - wide), 0.0)
    msg[0:STATE, :] = lax.dot_general(
        b_ref[...].astype(F32),
        scaled * to_end,
        (((0,), (0,)), ((), ())),
        preferred_element_type=F32,
        precision=HIGH,
    )
    keep = jnp.where(seg_last == seg_before, jnp.exp(last), 0.0)
    msg[STATE : STATE + 8, :] = jnp.broadcast_to(keep, (8, CHANNELS))


def chip_kernel(pair, out):
    keep = [pair[k, STATE : STATE + 1, :] for k in range(NC)]
    out[0:STATE, :] = (keep[1] * pair[0, 0:STATE, :] + pair[1, 0:STATE, :]).astype(BF16)
    both = keep[0] * keep[1]
    coarse = both.astype(BF16).astype(F32)
    line = lax.broadcasted_iota(jnp.int32, (MSG - STATE, CHANNELS), 0)
    out[STATE:MSG, :] = jnp.where(line == 0, coarse, jnp.where(line == 1, both - coarse, 0.0)).astype(
        BF16
    )


def gate_kernel(place, chips, pair, c_ref, inner, carry, gate, out):
    y, core = (place[1], place[2])
    state = jnp.zeros((STATE, CHANNELS), F32)
    for k in range(NY - 1):
        tail = chips[k, STATE:MSG, :].astype(F32)
        keep = tail[0:1, :] + tail[1:2, :]
        state = jnp.where(k < y, keep * state + chips[k, 0:STATE, :].astype(F32), state)
    state = jnp.where(
        core == 1, pair[0, STATE : STATE + 1, :] * state + pair[0, 0:STATE, :], state
    )
    ssd = inner[...] + carry[...] * dot(c_ref[...].astype(F32), state, HIGH)
    v = gate[...].astype(F32)
    out[...] = (ssd * (v / (1.0 + jnp.exp(-v)))).astype(BF16)


def square_kernel(rows, out):
    lane = lax.broadcasted_iota(jnp.int32, (ROWS, ROWS), 1)
    table = jnp.zeros((ROWS, ROWS), F32)
    for g in range(NG):
        v = rows[g].astype(F32)
        table = jnp.where(lane == g, jnp.sum(v * v, axis=1, keepdims=True), table)
    line = table.T[0:NG, :]
    for k in range(NL * NX):
        out[k] = line


def project_kernel(place, mine, paired, squares, gain, same, other, out):
    side = place[6]
    total = squares[0]
    for k in range(1, NL * NX):
        total = total + squares[k]
    scale = lax.rsqrt(total / 2048.0 + EPS)
    scale = jnp.concatenate([scale] * (ROWS // NG), axis=0).T
    result = jnp.zeros((ROWS, NX * ROWS), F32)
    lane = lax.broadcasted_iota(jnp.int32, (ROWS, ROWS), 1)
    for c, weight in enumerate((same, other)):
        core = lax.rem(place[2] + c, NC)
        for j in range(NY):
            g = j * NC + core
            column = jnp.sum(jnp.where(lane == g, scale, 0.0), axis=1, keepdims=True)
            for rows, half in ((mine, side), (paired, 1 - side)):
                line = (NL * g + half) * NX + place[4]
                normed = (rows[g].astype(F32) * column * gain[pl.ds(line, 1), :]).astype(BF16)
                block = jnp.concatenate([weight[j, k, half] for k in range(NX)], axis=1)
                result = result + dot(normed, block)
    for k in range(NX):
        out[k] = result[:, k * ROWS : (k + 1) * ROWS].astype(BF16)


def residual_kernel(parts, residual, mixer_out, summed):
    terms = [parts[k].astype(F32) for k in range(NX)]
    mixed = ((terms[0] + terms[1]) + (terms[2] + terms[3])).astype(BF16)
    mixer_out[...] = mixed
    summed[...] = (residual[...].astype(F32) + mixed.astype(F32)).astype(BF16)


def scaled_blocks(parts, sources, gain, g, square):
    blocks = []
    for part, source in zip(parts, sources):
        for half in range(NL):
            v = part[NL * g + half].astype(F32)
            square = square + v * v
            blocks.append((v * gain[NL * g + half, source]).astype(BF16))
    return jnp.concatenate(blocks, axis=1), square


def own_kernel(place, part, gain, weight, total, squares, later, held, arrived):
    copies = []
    for k in range(NX):
        source = lax.rem(place[4] + NX - k, NX)
        for g in range(NG):
            for half in range(NL):
                target = later.at[g, k - 1, half] if k else held.at[g, half]
                copies.append(
                    pltpu.make_async_copy(
                        weight.at[g, half, source], target, arrived.at[k, g, half]
                    )
                )
                copies[-1].start()
    result = jnp.zeros(total.shape, F32)
    square = jnp.zeros(squares.shape, F32)
    for g in range(NG):
        rows, square = scaled_blocks([part], [place[4]], gain, g, square)
        for half in range(NL):
            copies[NL * g + half].wait()
        result = result + dot(rows, jnp.concatenate([held[g, h] for h in range(NL)], axis=0))
    total[...] = result
    squares[...] = square
    for copy in copies[NG * NL :]:
        copy.wait()


def rest_kernel(place, p1, p2, p3, gain, weight, total, squares, wanted, out):
    parts = (p1, p2, p3)
    sources = [lax.rem(place[4] + NX - k, NX) for k in range(1, NX)]
    result = total[...]
    square = squares[...]
    for g in range(NG):
        rows, square = scaled_blocks(parts, sources, gain, g, square)
        pieces = [weight[g, k, half] for k in range(NX - 1) for half in range(NL)]
        result = result + dot(rows, jnp.concatenate(pieces, axis=0))
    mean = jnp.sum(square, axis=1, keepdims=True) / 8192.0
    logits = result * lax.rsqrt(mean + EPS)
    top = jnp.max(logits, axis=1, keepdims=True)
    mass = jnp.sum(jnp.exp(logits - top), axis=1, keepdims=True)
    begin = place[5] * logits.shape[1]
    vocab = begin + lax.broadcasted_iota(jnp.int32, logits.shape, 1)
    picked = jnp.sum(jnp.where(vocab == wanted[...], logits, 0.0), axis=1, keepdims=True)
    lane = lax.broadcasted_iota(jnp.int32, (ROWS, ROWS), 1)
    out[...] = jnp.where(lane % 2 == 0, top + jnp.log(mass), picked).T


def head(place, parts, gain, weight, wanted):
    columns = weight.shape[-1]
    square = jax.ShapeDtypeStruct((ROWS, ROWS), F32)
    cost = pl.CostEstimate(
        flops=2 * ROWS * NZ * ROWS * columns, bytes_accessed=1 << 24, transcendentals=0
    )
    params = pltpu.CompilerParams(vmem_limit_bytes=32 * 1024 * 1024)
    total, squares, later = pl.pallas_call(
        own_kernel,
        out_shape=(
            jax.ShapeDtypeStruct((ROWS, columns), F32),
            square,
            jax.ShapeDtypeStruct((NG, NX - 1, NL, ROWS, columns), BF16),
        ),
        in_specs=[smem(), vmem(), vmem(), pl.BlockSpec(memory_space=pl.ANY)],
        out_specs=[vmem()] * 3,
        scratch_shapes=[
            pltpu.VMEM((NG, NL, ROWS, columns), BF16),
            pltpu.SemaphoreType.DMA((NX, NG, NL)),
        ],
        cost_estimate=cost,
        compiler_params=params,
    )(place, parts[0], gain, weight)
    return pl.pallas_call(
        rest_kernel,
        out_shape=square,
        in_specs=[smem()] + [vmem()] * (NX + 4),
        out_specs=vmem(),
        cost_estimate=cost,
        compiler_params=params,
    )(place, *parts[1:], gain, later, total, squares, wanted)


def token_kernel(place, stats, seg, mask, logp, sums):
    even = lax.broadcasted_iota(jnp.int32, (ROWS, ROWS), 0) % 2 == 0
    table = stats[...]
    least = jnp.where(even, table, -jnp.inf)
    top = jnp.max(least, axis=0, keepdims=True)
    mass = jnp.sum(jnp.where(even, jnp.exp(least - top), 0.0), axis=0, keepdims=True)
    picked = jnp.sum(jnp.where(even, 0.0, table), axis=0, keepdims=True)
    value = picked - (top + jnp.log(mass))
    logp[...] = value
    mine = pl.ds(place[0], 1)
    counted = mask[mine, :] == 1
    lane = lax.broadcasted_iota(jnp.int32, (8, ROWS), 1)
    both = jnp.zeros((8, ROWS), F32)
    for k in range(2):
        chosen = jnp.where(counted & (seg[mine, :] == k), value, 0.0)
        both = jnp.where(lane == k, jnp.sum(chosen, axis=1, keepdims=True), both)
    sums[...] = both


def mean_kernel(sums, seg, mask, out):
    every = jnp.sum(sums[...], axis=0, keepdims=True)
    means = []
    for k in range(2):
        count = jnp.sum(jnp.where((mask[...] == 1) & (seg[...] == k), 1.0, 0.0))
        means.append(every[:, k : k + 1] / count)
    lane = lax.broadcasted_iota(jnp.int32, (1, ROWS), 1)
    out[...] = jnp.where(
        lane == 0, means[0], jnp.where(lane == 1, means[1], means[0] - means[1])
    )


def shifted(part, axis, k):
    n = lax.axis_size(axis)
    return lax.ppermute(part, axis, [(i, (i + k) % n) for i in range(n)])


def local(
    residual_in,
    ssm_input,
    gate_input,
    b_proj,
    c_proj,
    step_raw,
    decay_log,
    skip_gain,
    mixer_gain,
    out_weight,
    final_gain,
    head_weight,
    targets,
    segment_ids,
    loss_mask,
):
    y, core, zl, x = [lax.axis_index(axis) for axis in ("y", "core", "zl", "x")]
    group = lax.axis_index("zg")
    z = group * NL + zl
    seq = y * NC + core
    place = jnp.stack([seq, y, core, z, x, z * NX + x, zl]).astype(jnp.int32)
    seg = segment_ids.reshape(-1, ROWS)
    mask = loss_mask.reshape(-1, ROWS)
    b_rows = lax.dynamic_index_in_dim(b_proj, group, 1, keepdims=False)
    c_rows = lax.dynamic_index_in_dim(c_proj, group, 1, keepdims=False)

    rows = out_weight.reshape(1, NL, NX, CHANNELS, ROWS).transpose(0, 2, 1, 3, 4)
    rows = jnp.broadcast_to(rows, (NY, *rows.shape[1:])).reshape(NY * NX, NL, CHANNELS, ROWS)
    rows, b_rows = lax.optimization_barrier((rows, b_rows))
    inner, carry, msg = call(
        scan_kernel,
        (
            jax.ShapeDtypeStruct((ROWS, CHANNELS), F32),
            jax.ShapeDtypeStruct((ROWS, CHANNELS), F32),
            jax.ShapeDtypeStruct((STATE + 8, CHANNELS), F32),
        ),
        [smem()] + [vmem()] * 7,
    )(
        place,
        seg,
        step_raw.T,
        decay_log.reshape(1, HEADS),
        skip_gain.reshape(1, HEADS),
        ssm_input,
        b_rows,
        c_rows,
    )
    pair = lax.all_gather(msg, "core")
    chip = call(chip_kernel, jax.ShapeDtypeStruct((MSG, CHANNELS), BF16), [vmem()])(pair)
    chips = lax.all_gather(chip, "y")
    gated = call(
        gate_kernel, jax.ShapeDtypeStruct((ROWS, CHANNELS), BF16), [smem()] + [vmem()] * 6
    )(place, chips, pair, c_rows, inner, carry, gate_input)
    rows, weight, gated = lax.optimization_barrier((rows, head_weight, gated))
    same = lax.all_to_all(rows, ("y", "x"), 0, 0).reshape(NY, NX, NL, CHANNELS, ROWS)
    head_rows = lax.all_gather(weight, SEQ)
    mine = lax.all_gather(gated, "zg")
    odd = range(1, NZ, NL)
    swaps = [(i, (i + 1) % NZ) for i in odd] + [((i + 1) % NZ, i) for i in odd]
    same, mine = lax.optimization_barrier((same, mine))
    other = shifted(same, "core", 1)
    paired = lax.ppermute(mine, ("zg", "zl"), swaps)
    squares = call(
        square_kernel, jax.ShapeDtypeStruct((NL * NX, NG, ROWS), F32), [vmem()]
    )(mine)
    squares = lax.all_to_all(squares, ("zl", "x"), 0, 0)
    parts = call(
        project_kernel, jax.ShapeDtypeStruct((NX, ROWS, ROWS), BF16), [smem()] + [vmem()] * 6
    )(place, mine, paired, squares, mixer_gain.reshape(-1, CHANNELS), same, other)
    parts = lax.all_to_all(parts, "x", 0, 0)
    half = jax.ShapeDtypeStruct((ROWS, ROWS), BF16)
    mixer_out, summed = call(residual_kernel, (half, half), [vmem()] * 2)(parts, residual_in)

    column = lax.all_gather(summed, ("zg", "zl"))
    features = [column] + [shifted(column, "x", k) for k in range(1, NX)]
    wanted = lax.dynamic_slice_in_dim(targets, seq * ROWS, ROWS).reshape(ROWS, 1)
    gains = final_gain.reshape(NZ, NX, 1, ROWS)
    matrix = head_rows.reshape(NG, NL, NX, ROWS, -1)
    stats = head(place, features, gains, matrix, wanted)
    stats = lax.all_to_all(stats, MP, 0, 0, tiled=True)
    logp, sums = call(
        token_kernel,
        (jax.ShapeDtypeStruct((1, ROWS), F32), jax.ShapeDtypeStruct((8, ROWS), F32)),
        [smem()] + [vmem()] * 3,
    )(place, stats, seg, mask)
    sums = lax.all_to_all(sums, SEQ, 0, 0, tiled=True)
    means = call(mean_kernel, jax.ShapeDtypeStruct((1, ROWS), F32), [vmem()] * 3)(sums, seg, mask)
    return (mixer_out, logp.reshape(ROWS), means[0, :3])


def solution(mesh):
    fine = Mesh(mesh.devices.reshape(NY, NC, NG, NL, NX), AXES)
    mp = MP
    in_specs = (
        P(SEQ, mp),
        P(SEQ, mp),
        P(SEQ, mp),
        P(SEQ, None, None),
        P(SEQ, None, None),
        P(SEQ, mp),
        P(mp),
        P(mp),
        P(),
        P(SEQ, mp),
        P(),
        P(SEQ, mp),
        P(),
        P(),
        P(),
    )
    out_specs = (P(SEQ, mp), P(SEQ), P())
    return jax.shard_map(local, mesh=fine, in_specs=in_specs, out_specs=out_specs, check_vma=False)
```

```python
import jax
import jax.numpy as jnp
from jax import lax
from jax.experimental import pallas as pl
from jax.experimental.pallas import tpu as pltpu
from jax.sharding import Mesh, PartitionSpec as P

EPS = 1e-05
HIGH = lax.Precision.HIGHEST
F32 = jnp.float32
BF16 = jnp.bfloat16

NY, NC, NG, NL, NX = (4, 2, 8, 2, 4)
NZ = NG * NL
AXES = ("y", "core", "zg", "zl", "x")
SEQ = ("y", "core")
MP = ("zg", "zl", "x")
ROWS = 128
HEADS = 4
WIDTH = 64
CHANNELS = HEADS * WIDTH
STATE = 256
GROUPS = 8
MSG = STATE + 16
ORDER = (0, 2, 1, 3)


def dot(a, b, precision=None):
    return jnp.dot(a, b, preferred_element_type=F32, precision=precision)


def vmem():
    return pl.BlockSpec(memory_space=pltpu.VMEM)


def smem():
    return pl.BlockSpec(memory_space=pltpu.SMEM)


def call(body, out_shape, specs):
    many = isinstance(out_shape, (tuple, list))
    return pl.pallas_call(
        body,
        out_shape=out_shape,
        in_specs=specs,
        out_specs=[vmem() for _ in out_shape] if many else vmem(),
        compiler_params=pltpu.CompilerParams(vmem_limit_bytes=32 * 1024 * 1024),
    )


def head_columns(columns):
    lane = lax.broadcasted_iota(jnp.int32, (ROWS, CHANNELS), 1) // WIDTH
    wide = jnp.broadcast_to(columns[0], (ROWS, CHANNELS))
    for h in range(1, HEADS):
        wide = jnp.where(lane == h, columns[h], wide)
    return wide


def scan_kernel(place, seg, step_raw, decay_log, skip, x_ref, b_ref, c_ref, inner, carry, msg):
    row_start = place[0] * ROWS
    boundary = seg.shape[0] * seg.shape[1] - jnp.sum(seg[...])
    raw = jnp.concatenate([step_raw[...]] * (ROWS // HEADS), axis=0).T[:, 0:HEADS]
    step = jnp.maximum(raw, 0.0) + jnp.log1p(jnp.exp(-jnp.abs(raw)))
    log_decay = -jnp.exp(decay_log[...]) * step
    share = ROWS // HEADS
    lane = lax.broadcasted_iota(jnp.int32, (ROWS, ROWS), 1)
    row = lax.broadcasted_iota(jnp.int32, (ROWS, ROWS), 0)
    spread = jnp.broadcast_to(log_decay[:, 0:1], (ROWS, ROWS))
    for h in range(1, HEADS):
        spread = jnp.where(lane // share == h, log_decay[:, h : h + 1], spread)
    below = (row >= lane).astype(F32)
    total = dot(below, spread, HIGH)
    total_t = total.T
    columns = [total[:, share * h : share * h + 1] for h in range(HEADS)]
    wide = head_columns(columns)
    places = row_start + lax.broadcasted_iota(jnp.int32, (ROWS, 1), 0)
    seg_rows = (places >= boundary).astype(jnp.int32)
    seg_lanes = (row_start + lane >= boundary).astype(jnp.int32)
    seg_before = (jnp.maximum(row_start - 1, 0) >= boundary).astype(jnp.int32)
    seg_last = (row_start + ROWS - 1 >= boundary).astype(jnp.int32)
    allowed = (row >= lane) & (seg_rows == seg_lanes)
    inputs = x_ref[...].astype(F32)
    scaled = head_columns([step[:, h : h + 1] for h in range(HEADS)]) * inputs
    scores = lax.dot_general(
        c_ref[...], b_ref[...], (((1,), (1,)), ((), ())), preferred_element_type=F32
    )
    for h in range(HEADS):
        gap = columns[h] - total_t[share * h : share * h + 1, :]
        weight = jnp.where(allowed, jnp.exp(jnp.where(allowed, gap, 0.0)), 0.0)
        part = slice(h * WIDTH, (h + 1) * WIDTH)
        inner[:, part] = dot(scores * weight, scaled[:, part], HIGH)
    gains = jnp.broadcast_to(skip[...], (ROWS, HEADS))
    inner[...] += head_columns([gains[:, h : h + 1] for h in range(HEADS)]) * inputs
    carry[...] = jnp.where(seg_rows == seg_before, jnp.exp(wide), 0.0)
    last = wide[ROWS - 1 : ROWS, :]
    to_end = jnp.where(seg_rows == seg_last, jnp.exp(last - wide), 0.0)
    msg[0:STATE, :] = lax.dot_general(
        b_ref[...].astype(F32),
        scaled * to_end,
        (((0,), (0,)), ((), ())),
        preferred_element_type=F32,
        precision=HIGH,
    )
    keep = jnp.where(seg_last == seg_before, jnp.exp(last), 0.0)
    msg[STATE : STATE + 8, :] = jnp.broadcast_to(keep, (8, CHANNELS))


def chip_kernel(pair, out):
    keep = [pair[k, STATE : STATE + 1, :] for k in range(NC)]
    out[0:STATE, :] = (keep[1] * pair[0, 0:STATE, :] + pair[1, 0:STATE, :]).astype(BF16)
    both = keep[0] * keep[1]
    coarse = both.astype(BF16).astype(F32)
    line = lax.broadcasted_iota(jnp.int32, (MSG - STATE, CHANNELS), 0)
    out[STATE:MSG, :] = jnp.where(line == 0, coarse, jnp.where(line == 1, both - coarse, 0.0)).astype(
        BF16
    )


def gate_kernel(place, chips, pair, c_ref, inner, carry, gate, out):
    y, core = (place[1], place[2])
    state = jnp.zeros((STATE, CHANNELS), F32)
    for k in range(NY - 1):
        tail = chips[k, STATE:MSG, :].astype(F32)
        keep = tail[0:1, :] + tail[1:2, :]
        state = jnp.where(k < y, keep * state + chips[k, 0:STATE, :].astype(F32), state)
    state = jnp.where(
        core == 1, pair[0, STATE : STATE + 1, :] * state + pair[0, 0:STATE, :], state
    )
    ssd = inner[...] + carry[...] * dot(c_ref[...].astype(F32), state, HIGH)
    v = gate[...].astype(F32)
    out[...] = (ssd * (v / (1.0 + jnp.exp(-v)))).astype(BF16)


def square_kernel(rows, out):
    lane = lax.broadcasted_iota(jnp.int32, (ROWS, ROWS), 1)
    table = jnp.zeros((ROWS, ROWS), F32)
    for g in range(NG):
        v = rows[g].astype(F32)
        table = jnp.where(lane == g, jnp.sum(v * v, axis=1, keepdims=True), table)
    line = table.T[0:NG, :]
    for k in range(NL * NX):
        out[k] = line


def project_kernel(place, mine, paired, squares, gain, same, other, out):
    side = place[6]
    total = squares[0]
    for k in range(1, NL * NX):
        total = total + squares[k]
    scale = lax.rsqrt(total / 2048.0 + EPS)
    scale = jnp.concatenate([scale] * (ROWS // NG), axis=0).T
    result = jnp.zeros((ROWS, NX * ROWS), F32)
    lane = lax.broadcasted_iota(jnp.int32, (ROWS, ROWS), 1)
    for c, weight in enumerate((same, other)):
        core = lax.rem(place[2] + c, NC)
        for j in range(NY):
            g = j * NC + core
            column = jnp.sum(jnp.where(lane == g, scale, 0.0), axis=1, keepdims=True)
            for rows, half in ((mine, side), (paired, 1 - side)):
                line = (NL * g + half) * NX + place[4]
                normed = (rows[g].astype(F32) * column * gain[pl.ds(line, 1), :]).astype(BF16)
                block = jnp.concatenate([weight[j, k, half] for k in range(NX)], axis=1)
                result = result + dot(normed, block)
    for k in range(NX):
        out[k] = result[:, k * ROWS : (k + 1) * ROWS]


def residual_kernel(parts, residual, mixer_out, summed):
    mixed = ((parts[0] + parts[1]) + (parts[2] + parts[3])).astype(BF16)
    mixer_out[...] = mixed
    summed[...] = (residual[...].astype(F32) + mixed.astype(F32)).astype(BF16)


def scaled_blocks(parts, sources, gain, g, square):
    blocks = []
    for part, source in zip(parts, sources):
        for half in range(NL):
            v = part[NL * g + half].astype(F32)
            square = square + v * v
            blocks.append((v * gain[NL * g + half, source]).astype(BF16))
    return jnp.concatenate(blocks, axis=1), square


def own_kernel(place, part, gain, weight, total, squares, later, held, arrived):
    copies = []
    for k in range(NX):
        source = lax.rem(place[4] + NX - ORDER[k], NX)
        for g in range(NG):
            for half in range(NL):
                target = later.at[g, k - 1, half] if k else held.at[g, half]
                copies.append(
                    pltpu.make_async_copy(
                        weight.at[g, half, source], target, arrived.at[k, g, half]
                    )
                )
                copies[-1].start()
    result = jnp.zeros(total.shape, F32)
    square = jnp.zeros(squares.shape, F32)
    for g in range(NG):
        rows, square = scaled_blocks([part], [place[4]], gain, g, square)
        for half in range(NL):
            copies[NL * g + half].wait()
        result = result + dot(rows, jnp.concatenate([held[g, h] for h in range(NL)], axis=0))
    total[...] = result
    squares[...] = square
    for copy in copies[NG * NL :]:
        copy.wait()


def rest_kernel(place, p1, p2, p3, gain, weight, total, squares, wanted, out):
    parts = (p1, p2, p3)
    sources = [lax.rem(place[4] + NX - k, NX) for k in ORDER[1:]]
    result = total[...]
    square = squares[...]
    for g in range(NG):
        rows, square = scaled_blocks(parts, sources, gain, g, square)
        pieces = [weight[g, k, half] for k in range(NX - 1) for half in range(NL)]
        result = result + dot(rows, jnp.concatenate(pieces, axis=0))
    mean = jnp.sum(square, axis=1, keepdims=True) / 8192.0
    logits = result * lax.rsqrt(mean + EPS)
    top = jnp.max(logits, axis=1, keepdims=True)
    mass = jnp.sum(jnp.exp(logits - top), axis=1, keepdims=True)
    begin = place[5] * logits.shape[1]
    vocab = begin + lax.broadcasted_iota(jnp.int32, logits.shape, 1)
    picked = jnp.sum(jnp.where(vocab == wanted[...], logits, 0.0), axis=1, keepdims=True)
    lane = lax.broadcasted_iota(jnp.int32, (ROWS, ROWS), 1)
    out[...] = jnp.where(lane % 2 == 0, top + jnp.log(mass), picked).T


def head(place, parts, gain, weight, wanted):
    columns = weight.shape[-1]
    square = jax.ShapeDtypeStruct((ROWS, ROWS), F32)
    cost = pl.CostEstimate(
        flops=2 * ROWS * NZ * ROWS * columns, bytes_accessed=1 << 24, transcendentals=0
    )
    params = pltpu.CompilerParams(vmem_limit_bytes=32 * 1024 * 1024)
    total, squares, later = pl.pallas_call(
        own_kernel,
        out_shape=(
            jax.ShapeDtypeStruct((ROWS, columns), F32),
            square,
            jax.ShapeDtypeStruct((NG, NX - 1, NL, ROWS, columns), BF16),
        ),
        in_specs=[smem(), vmem(), vmem(), pl.BlockSpec(memory_space=pl.ANY)],
        out_specs=[vmem()] * 3,
        scratch_shapes=[
            pltpu.VMEM((NG, NL, ROWS, columns), BF16),
            pltpu.SemaphoreType.DMA((NX, NG, NL)),
        ],
        cost_estimate=cost,
        compiler_params=params,
    )(place, parts[0], gain, weight)
    return pl.pallas_call(
        rest_kernel,
        out_shape=square,
        in_specs=[smem()] + [vmem()] * (NX + 4),
        out_specs=vmem(),
        cost_estimate=cost,
        compiler_params=params,
    )(place, *parts[1:], gain, later, total, squares, wanted)


def token_kernel(place, stats, seg, mask, logp, sums):
    even = lax.broadcasted_iota(jnp.int32, (ROWS, ROWS), 0) % 2 == 0
    table = stats[...]
    least = jnp.where(even, table, -jnp.inf)
    top = jnp.max(least, axis=0, keepdims=True)
    mass = jnp.sum(jnp.where(even, jnp.exp(least - top), 0.0), axis=0, keepdims=True)
    picked = jnp.sum(jnp.where(even, 0.0, table), axis=0, keepdims=True)
    value = picked - (top + jnp.log(mass))
    logp[...] = value
    mine = pl.ds(place[0], 1)
    counted = mask[mine, :] == 1
    lane = lax.broadcasted_iota(jnp.int32, (8, ROWS), 1)
    both = jnp.zeros((8, ROWS), F32)
    for k in range(2):
        chosen = jnp.where(counted & (seg[mine, :] == k), value, 0.0)
        both = jnp.where(lane == k, jnp.sum(chosen, axis=1, keepdims=True), both)
    sums[...] = both


def mean_kernel(sums, seg, mask, out):
    every = jnp.sum(sums[...], axis=0, keepdims=True)
    means = []
    for k in range(2):
        count = jnp.sum(jnp.where((mask[...] == 1) & (seg[...] == k), 1.0, 0.0))
        means.append(every[:, k : k + 1] / count)
    lane = lax.broadcasted_iota(jnp.int32, (1, ROWS), 1)
    out[...] = jnp.where(
        lane == 0, means[0], jnp.where(lane == 1, means[1], means[0] - means[1])
    )


def shifted(part, axis, k):
    n = lax.axis_size(axis)
    return lax.ppermute(part, axis, [(i, (i + k) % n) for i in range(n)])


def local(
    residual_in,
    ssm_input,
    gate_input,
    b_proj,
    c_proj,
    step_raw,
    decay_log,
    skip_gain,
    mixer_gain,
    out_weight,
    final_gain,
    head_weight,
    targets,
    segment_ids,
    loss_mask,
):
    y, core, zl, x = [lax.axis_index(axis) for axis in ("y", "core", "zl", "x")]
    group = lax.axis_index("zg")
    z = group * NL + zl
    seq = y * NC + core
    place = jnp.stack([seq, y, core, z, x, z * NX + x, zl]).astype(jnp.int32)
    seg = segment_ids.reshape(-1, ROWS)
    mask = loss_mask.reshape(-1, ROWS)
    b_rows = lax.dynamic_index_in_dim(b_proj, group, 1, keepdims=False)
    c_rows = lax.dynamic_index_in_dim(c_proj, group, 1, keepdims=False)

    rows = out_weight.reshape(1, NL, NX, CHANNELS, ROWS).transpose(0, 2, 1, 3, 4)
    rows = jnp.broadcast_to(rows, (NY, *rows.shape[1:])).reshape(NY * NX, NL, CHANNELS, ROWS)
    rows, b_rows = lax.optimization_barrier((rows, b_rows))
    inner, carry, msg = call(
        scan_kernel,
        (
            jax.ShapeDtypeStruct((ROWS, CHANNELS), F32),
            jax.ShapeDtypeStruct((ROWS, CHANNELS), F32),
            jax.ShapeDtypeStruct((STATE + 8, CHANNELS), F32),
        ),
        [smem()] + [vmem()] * 7,
    )(
        place,
        seg,
        step_raw.T,
        decay_log.reshape(1, HEADS),
        skip_gain.reshape(1, HEADS),
        ssm_input,
        b_rows,
        c_rows,
    )
    pair = lax.all_gather(msg, "core")
    chip = call(chip_kernel, jax.ShapeDtypeStruct((MSG, CHANNELS), BF16), [vmem()])(pair)
    chips = lax.all_gather(chip, "y")
    gated = call(
        gate_kernel, jax.ShapeDtypeStruct((ROWS, CHANNELS), BF16), [smem()] + [vmem()] * 6
    )(place, chips, pair, c_rows, inner, carry, gate_input)
    rows, weight, gated = lax.optimization_barrier((rows, head_weight, gated))
    same = lax.all_to_all(rows, ("y", "x"), 0, 0).reshape(NY, NX, NL, CHANNELS, ROWS)
    head_rows = lax.all_gather(weight, SEQ)
    mine = lax.all_gather(gated, "zg")
    odd = range(1, NZ, NL)
    swaps = [(i, (i + 1) % NZ) for i in odd] + [((i + 1) % NZ, i) for i in odd]
    same, mine = lax.optimization_barrier((same, mine))
    other = shifted(same, "core", 1)
    paired = lax.ppermute(mine, ("zg", "zl"), swaps)
    squares = call(
        square_kernel, jax.ShapeDtypeStruct((NL * NX, NG, ROWS), F32), [vmem()]
    )(mine)
    squares = lax.all_to_all(squares, ("zl", "x"), 0, 0)
    parts = call(
        project_kernel, jax.ShapeDtypeStruct((NX, ROWS, ROWS), F32), [smem()] + [vmem()] * 6
    )(place, mine, paired, squares, mixer_gain.reshape(-1, CHANNELS), same, other)
    parts = lax.all_to_all(parts, "x", 0, 0)
    half = jax.ShapeDtypeStruct((ROWS, ROWS), BF16)
    mixer_out, summed = call(residual_kernel, (half, half), [vmem()] * 2)(parts, residual_in)

    column = lax.all_gather(summed, ("zg", "zl"))
    features = [column] + [shifted(column, "x", k) for k in ORDER[1:]]
    wanted = lax.dynamic_slice_in_dim(targets, seq * ROWS, ROWS).reshape(ROWS, 1)
    gains = final_gain.reshape(NZ, NX, 1, ROWS)
    matrix = head_rows.reshape(NG, NL, NX, ROWS, -1)
    stats = head(place, features, gains, matrix, wanted)
    stats = lax.all_to_all(stats, MP, 0, 0, tiled=True)
    logp, sums = call(
        token_kernel,
        (jax.ShapeDtypeStruct((1, ROWS), F32), jax.ShapeDtypeStruct((8, ROWS), F32)),
        [smem()] + [vmem()] * 3,
    )(place, stats, seg, mask)
    sums = lax.all_to_all(sums, SEQ, 0, 0, tiled=True)
    means = call(mean_kernel, jax.ShapeDtypeStruct((1, ROWS), F32), [vmem()] * 3)(sums, seg, mask)
    return (mixer_out, logp.reshape(ROWS), means[0, :3])


def solution(mesh):
    fine = Mesh(mesh.devices.reshape(NY, NC, NG, NL, NX), AXES)
    mp = MP
    in_specs = (
        P(SEQ, mp),
        P(SEQ, mp),
        P(SEQ, mp),
        P(SEQ, None, None),
        P(SEQ, None, None),
        P(SEQ, mp),
        P(mp),
        P(mp),
        P(),
        P(SEQ, mp),
        P(),
        P(SEQ, mp),
        P(),
        P(),
        P(),
    )
    out_specs = (P(SEQ, mp), P(SEQ), P())
    return jax.shard_map(local, mesh=fine, in_specs=in_specs, out_specs=out_specs, check_vma=False)
```
